32 devices in a mesh: tensor: 4 (over y, x), dp: 8 (over z, core).
Axes of the slice: x: 2, y: 2, z: 4, core: 2. Of those that a mesh axis runs over, the one named last changes fastest.
Arguments:
- inputs: float32 [3072, 1024], P('dp'), may hold values from -6 to 6
- cotangent: float32 [3072, 1024], P('dp'), may hold values from -6 to 6
- norm_gains: float32 [2, 1024], replicated, may hold values from 0.5 to 1.5
- mix_weight: float32 [1024, 8, 768], P('dp', 'tensor'), may hold values from -0.1875 to 0.1875
- gate_weight: float32 [1024, 2, 8], P('dp', None, 'tensor'), may hold values from -0.1875 to 0.1875
- conv_weight: float32 [4, 8, 512], P(None, 'tensor'), may hold values from -3 to 3
- a_log: float32 [8], P('tensor'), may hold values from -4 to 1
- dt_bias: float32 [8], P('tensor'), may hold values from -4 to -1
- out_gain: float32 [256], replicated, may hold values from 0.5 to 1.5
- out_weight: float32 [8, 256, 1024], P('tensor', None, 'dp'), may hold values from -0.25 to 0.25
- upgate_weight: float32 [1024, 2, 2816], P('dp', None, 'tensor'), may hold values from -0.1875 to 0.1875
- down_weight: float32 [2816, 1024], P('tensor', 'dp'), may hold values from -0.21875 to 0.21875
- moment_norm_gains: float32 [2, 1024], replicated, may hold values from -4 to 4
- moment_mix_weight: float32 [1024, 8, 768], P('dp', 'tensor'), may hold values from -4 to 4
- moment_gate_weight: float32 [1024, 2, 8], P('dp', None, 'tensor'), may hold values from -4 to 4
- moment_conv_weight: float32 [4, 8, 512], P(None, 'tensor'), may hold values from -4 to 4
- moment_a_log: float32 [8], P('tensor'), may hold values from -4 to 4
- moment_dt_bias: float32 [8], P('tensor'), may hold values from -4 to 4
- moment_out_gain: float32 [256], replicated, may hold values from -4 to 4
- moment_out_weight: float32 [8, 256, 1024], P('tensor', None, 'dp'), may hold values from -4 to 4
- moment_upgate_weight: float32 [1024, 2, 2816], P('dp', None, 'tensor'), may hold values from -4 to 4
- moment_down_weight: float32 [2816, 1024], P('tensor', 'dp'), may hold values from -4 to 4
- second_norm_gains: float32 [2, 1024], replicated, may hold values from 0.005 to 0.02
- second_mix_weight: float32 [1024, 8, 768], P('dp', 'tensor'), may hold values from 0.005 to 0.02
- second_gate_weight: float32 [1024, 2, 8], P('dp', None, 'tensor'), may hold values from 0.005 to 0.02
- second_conv_weight: float32 [4, 8, 512], P(None, 'tensor'), may hold values from 0.005 to 0.02
- second_a_log: float32 [8], P('tensor'), may hold values from 0.005 to 0.02
- second_dt_bias: float32 [8], P('tensor'), may hold values from 0.005 to 0.02
- second_out_gain: float32 [256], replicated, may hold values from 0.005 to 0.02
- second_out_weight: float32 [8, 256, 1024], P('tensor', None, 'dp'), may hold values from 0.005 to 0.02
- second_upgate_weight: float32 [1024, 2, 2816], P('dp', None, 'tensor'), may hold values from 0.005 to 0.02
- second_down_weight: float32 [2816, 1024], P('tensor', 'dp'), may hold values from 0.005 to 0.02
Outputs:
- outputs: float32 [3072, 1024], P('dp')
- grad_inputs: float32 [3072, 1024], P('dp')
- grad_norm_gains: float32 [2, 1024], replicated
- grad_mix_weight: float32 [1024, 8, 768], P('dp', 'tensor')
- grad_gate_weight: float32 [1024, 2, 8], P('dp', None, 'tensor')
- grad_conv_weight: float32 [4, 8, 512], P(None, 'tensor')
- grad_a_log: float32 [8], P('tensor')
- grad_dt_bias: float32 [8], P('tensor')
- grad_out_gain: float32 [256], replicated
- grad_out_weight: float32 [8, 256, 1024], P('tensor', None, 'dp')
- grad_upgate_weight: float32 [1024, 2, 2816], P('dp', None, 'tensor')
- grad_down_weight: float32 [2816, 1024], P('tensor', 'dp')
- new_norm_gains: float32 [2, 1024], replicated
- new_mix_weight: float32 [1024, 8, 768], P('dp', 'tensor')
- new_gate_weight: float32 [1024, 2, 8], P('dp', None, 'tensor')
- new_conv_weight: float32 [4, 8, 512], P(None, 'tensor')
- new_a_log: float32 [8], P('tensor')
- new_dt_bias: float32 [8], P('tensor')
- new_out_gain: float32 [256], replicated
- new_out_weight: float32 [8, 256, 1024], P('tensor', None, 'dp')
- new_upgate_weight: float32 [1024, 2, 2816], P('dp', None, 'tensor')
- new_down_weight: float32 [2816, 1024], P('tensor', 'dp')
- new_moment_norm_gains: float32 [2, 1024], replicated
- new_moment_mix_weight: float32 [1024, 8, 768], P('dp', 'tensor')
- new_moment_gate_weight: float32 [1024, 2, 8], P('dp', None, 'tensor')
- new_moment_conv_weight: float32 [4, 8, 512], P(None, 'tensor')
- new_moment_a_log: float32 [8], P('tensor')
- new_moment_dt_bias: float32 [8], P('tensor')
- new_moment_out_gain: float32 [256], replicated
- new_moment_out_weight: float32 [8, 256, 1024], P('tensor', None, 'dp')
- new_moment_upgate_weight: float32 [1024, 2, 2816], P('dp', None, 'tensor')
- new_moment_down_weight: float32 [2816, 1024], P('tensor', 'dp')
- new_second_norm_gains: float32 [2, 1024], replicated
- new_second_mix_weight: float32 [1024, 8, 768], P('dp', 'tensor')
- new_second_gate_weight: float32 [1024, 2, 8], P('dp', None, 'tensor')
- new_second_conv_weight: float32 [4, 8, 512], P(None, 'tensor')
- new_second_a_log: float32 [8], P('tensor')
- new_second_dt_bias: float32 [8], P('tensor')
- new_second_out_gain: float32 [256], replicated
- new_second_out_weight: float32 [8, 256, 1024], P('tensor', None, 'dp')
- new_second_upgate_weight: float32 [1024, 2, 2816], P('dp', None, 'tensor')
- new_second_down_weight: float32 [2816, 1024], P('tensor', 'dp')
The draws below stay inside these ranges and needn't reach their ends.
All inputs are finite; a program needn't handle non-finite values.
Results may differ from the reference program's by a relative error of at most 0.02.
Values may be sent and summed in bfloat16 or wider, within the bound.
A program may use at most 192 MiB of HBM per device.

```python
import math
import jax
import jax.numpy as jnp
from jax import lax

D = 1024
H = 8
DK = 128
DV = 256
FF = 2816
CONV = 4
SPAN = 64
LEN = 384
STEP = 3
TOKENS = 3072


def steps_of(own_key, shape, cuts, low, largest):
    level, own = 1.0, jax.random.fold_in(own_key, 6)
    for position, parts in cuts:
        steps = jnp.exp(jax.random.uniform(jax.random.fold_in(own, position), (parts,), jnp.float32, low / len(cuts), largest / len(cuts)))
        level = level * jnp.repeat(steps, shape[position] // parts).reshape([-1 if axis == position else 1 for axis in range(len(shape))])
    return level


def noise(own_key, dims, scale, most, shards=(), kind=jnp.bfloat16):
    drawn = scale * jax.random.normal(own_key, dims, jnp.float32)
    if shards:
        drawn = drawn * steps_of(own_key, dims, shards, -0.22, 0.18)
    return jnp.clip(drawn, -most, most).astype(kind)


def setup_inputs(seed: int = 0) -> dict:
    seeds = jax.random.split(jax.random.key(seed), 33)
    inputs = noise(seeds[0], (TOKENS, D), 1.0, 6.0, ((0, 8),), jnp.float32)
    cotangent = noise(seeds[1], (TOKENS, D), 1.0, 6.0, ((0, 8),), jnp.float32)
    norm_gains = jnp.clip(1.0 + 0.1 * jax.random.normal(seeds[2], (2, D), jnp.float32), 0.5, 1.5)
    mix_weight = noise(seeds[3], (D, H, 2 * DK + 2 * DV), D ** -0.5, 0.1875, ((0, 8), (1, 4)), jnp.float32)
    gate_weight = noise(seeds[4], (D, 2, H), D ** -0.5, 0.1875, ((0, 8), (2, 4)), jnp.float32)
    conv_weight = noise(seeds[5], (CONV, H, 2 * DK + DV), CONV ** -0.5, 3.0, ((1, 4),), jnp.float32)
    a_log = jnp.clip(-4.0 + 5.0 * jax.random.uniform(seeds[6], (H,), jnp.float32) ** steps_of(seeds[6], (H,), ((0, 4),), -0.2, 0.2), -4.0, 1.0)
    dt_bias = jnp.clip(-4.0 + 3.0 * jax.random.uniform(seeds[7], (H,), jnp.float32) ** steps_of(seeds[7], (H,), ((0, 4),), -0.2, 0.2), -4.0, -1.0)
    out_gain = jnp.clip(1.0 + 0.1 * jax.random.normal(seeds[8], (DV,), jnp.float32), 0.5, 1.5)
    out_weight = noise(seeds[9], (H, DV, D), (H * DV // 4) ** -0.5, 0.25, ((0, 4), (2, 8)), jnp.float32)
    upgate_weight = noise(seeds[10], (D, 2, FF), D ** -0.5, 0.1875, ((0, 8), (2, 4)), jnp.float32)
    down_weight = noise(seeds[11], (FF, D), (FF // 4) ** -0.5, 0.21875, ((0, 4), (1, 8)), jnp.float32)
    moment_norm_gains = noise(seeds[12], (2, D), 0.3, 4.0, (), jnp.float32)
    moment_mix_weight = noise(seeds[13], (D, H, 2 * DK + 2 * DV), 0.3, 4.0, ((0, 8), (1, 4)), jnp.float32)
    moment_gate_weight = noise(seeds[14], (D, 2, H), 0.3, 4.0, ((0, 8), (2, 4)), jnp.float32)
    moment_conv_weight = noise(seeds[15], (CONV, H, 2 * DK + DV), 0.3, 4.0, ((1, 4),), jnp.float32)
    moment_a_log = noise(seeds[16], (H,), 0.3, 4.0, ((0, 4),), jnp.float32)
    moment_dt_bias = noise(seeds[17], (H,), 0.3, 4.0, ((0, 4),), jnp.float32)
    moment_out_gain = noise(seeds[18], (DV,), 0.3, 4.0, (), jnp.float32)
    moment_out_weight = noise(seeds[19], (H, DV, D), 0.3, 4.0, ((0, 4), (2, 8)), jnp.float32)
    moment_upgate_weight = noise(seeds[20], (D, 2, FF), 0.3, 4.0, ((0, 8), (2, 4)), jnp.float32)
    moment_down_weight = noise(seeds[21], (FF, D), 0.3, 4.0, ((0, 4), (1, 8)), jnp.float32)
    second_norm_gains = jnp.clip(jnp.exp(jax.random.uniform(seeds[22], (2, D), jnp.float32, math.log(0.005), math.log(0.02))), 0.005, 0.02)
    second_mix_weight = jnp.clip(jnp.exp(math.log(0.02) - 1.3862944 * jax.random.uniform(seeds[23], (D, H, 2 * DK + 2 * DV), jnp.float32) ** steps_of(seeds[23], (D, H, 2 * DK + 2 * DV), ((0, 8), (1, 4)), -0.2, 0.2)), 0.005, 0.02)
    second_gate_weight = jnp.clip(jnp.exp(math.log(0.02) - 1.3862944 * jax.random.uniform(seeds[24], (D, 2, H), jnp.float32) ** steps_of(seeds[24], (D, 2, H), ((0, 8), (2, 4)), -0.2, 0.2)), 0.005, 0.02)
    second_conv_weight = jnp.clip(jnp.exp(math.log(0.02) - 1.3862944 * jax.random.uniform(seeds[25], (CONV, H, 2 * DK + DV), jnp.float32) ** steps_of(seeds[25], (CONV, H, 2 * DK + DV), ((1, 4),), -0.2, 0.2)), 0.005, 0.02)
    second_a_log = jnp.clip(jnp.exp(math.log(0.02) - 1.3862944 * jax.random.uniform(seeds[26], (H,), jnp.float32) ** steps_of(seeds[26], (H,), ((0, 4),), -0.2, 0.2)), 0.005, 0.02)
    second_dt_bias = jnp.clip(jnp.exp(math.log(0.02) - 1.3862944 * jax.random.uniform(seeds[27], (H,), jnp.float32) ** steps_of(seeds[27], (H,), ((0, 4),), -0.2, 0.2)), 0.005, 0.02)
    second_out_gain = jnp.clip(jnp.exp(jax.random.uniform(seeds[28], (DV,), jnp.float32, math.log(0.005), math.log(0.02))), 0.005, 0.02)
    second_out_weight = jnp.clip(jnp.exp(math.log(0.02) - 1.3862944 * jax.random.uniform(seeds[29], (H, DV, D), jnp.float32) ** steps_of(seeds[29], (H, DV, D), ((0, 4), (2, 8)), -0.2, 0.2)), 0.005, 0.02)
    second_upgate_weight = jnp.clip(jnp.exp(math.log(0.02) - 1.3862944 * jax.random.uniform(seeds[30], (D, 2, FF), jnp.float32) ** steps_of(seeds[30], (D, 2, FF), ((0, 8), (2, 4)), -0.2, 0.2)), 0.005, 0.02)
    second_down_weight = jnp.clip(jnp.exp(math.log(0.02) - 1.3862944 * jax.random.uniform(seeds[31], (FF, D), jnp.float32) ** steps_of(seeds[31], (FF, D), ((0, 4), (1, 8)), -0.2, 0.2)), 0.005, 0.02)
    return dict(inputs=inputs, cotangent=cotangent, norm_gains=norm_gains, mix_weight=mix_weight, gate_weight=gate_weight, conv_weight=conv_weight, a_log=a_log, dt_bias=dt_bias, out_gain=out_gain, out_weight=out_weight, upgate_weight=upgate_weight, down_weight=down_weight, moment_norm_gains=moment_norm_gains, moment_mix_weight=moment_mix_weight, moment_gate_weight=moment_gate_weight, moment_conv_weight=moment_conv_weight, moment_a_log=moment_a_log, moment_dt_bias=moment_dt_bias, moment_out_gain=moment_out_gain, moment_out_weight=moment_out_weight, moment_upgate_weight=moment_upgate_weight, moment_down_weight=moment_down_weight, second_norm_gains=second_norm_gains, second_mix_weight=second_mix_weight, second_gate_weight=second_gate_weight, second_conv_weight=second_conv_weight, second_a_log=second_a_log, second_dt_bias=second_dt_bias, second_out_gain=second_out_gain, second_out_weight=second_out_weight, second_upgate_weight=second_upgate_weight, second_down_weight=second_down_weight)


HIGHEST = lax.Precision.HIGHEST
RATE_MATRIX = 0.01
RATE_VECTOR = 0.1
CLIP_SHARE = 0.3

def rms_scale(rows_in, gain_row, epsilon):
    return rows_in * lax.rsqrt(lax.optimization_barrier(jnp.mean(rows_in * rows_in, axis=-1, keepdims=True)) + epsilon) * gain_row

def norm_apply(rows_in, gain_row):
    return rms_scale(rows_in, gain_row, 1e-05)

def unit_rows(rows_in):
    return rows_in * lax.rsqrt(lax.optimization_barrier(jnp.sum(rows_in * rows_in, axis=-1, keepdims=True)) + 1e-06)

def swiglu(paired):
    return jax.nn.silu(paired[:, 0]) * paired[:, 1]

def inverse_unit_lower(lower_part):
    size_now = lower_part.shape[-1]
    identity = jnp.eye(size_now, dtype=jnp.float32)
    inverse = identity - lower_part
    power_now = jnp.matmul(lower_part, lower_part, precision=HIGHEST)
    for repeat in range(size_now.bit_length() - 2):
        inverse = jnp.matmul(inverse, identity + power_now, precision=HIGHEST)
        power_now = jnp.matmul(power_now, power_now, precision=HIGHEST)
    return inverse

def delta_rule(queries, keys_now, values_now, beta_gate, decays):
    seq_count, length, head_count, key_size = keys_now.shape
    value_size = values_now.shape[-1]
    block_count = length // SPAN

    def to_blocks(array_in):
        shaped = array_in.reshape((seq_count, block_count, SPAN, head_count) + array_in.shape[3:])
        return jnp.moveaxis(shaped, (1, 3), (0, 2))
    strict = jnp.tril(jnp.ones((SPAN, SPAN), bool), -1)
    inclusive = jnp.tril(jnp.ones((SPAN, SPAN), bool))

    def block_step(state, block_items):
        query_block, key_block, value_block, beta_block, decay_block = block_items
        cumulative = jnp.cumsum(decay_block, axis=-1)
        log_gaps = cumulative[..., :, None] - cumulative[..., None, :]
        fall_strict = jnp.where(strict, jnp.exp(jnp.where(strict, log_gaps, 0.0)), 0.0)
        fall_inclusive = jnp.where(inclusive, jnp.exp(jnp.where(inclusive, log_gaps, 0.0)), 0.0)
        keys_keys = jnp.einsum('shtk,shuk->shtu', key_block, key_block, precision=HIGHEST)
        lower_part = beta_block[..., :, None] * keys_keys * fall_strict
        inverse = inverse_unit_lower(lower_part)
        growth = jnp.exp(cumulative)
        carried = jnp.einsum('shtk,shkv->shtv', key_block, state, precision=HIGHEST)
        right_side = beta_block[..., None] * (value_block - growth[..., None] * carried)
        new_values = jnp.einsum('shtu,shuv->shtv', inverse, right_side, precision=HIGHEST)
        scores = jnp.einsum('shtk,shuk->shtu', query_block, key_block, precision=HIGHEST) * fall_inclusive
        block_out = growth[..., None] * jnp.einsum('shtk,shkv->shtv', query_block, state, precision=HIGHEST)
        block_out = block_out + jnp.einsum('shtu,shuv->shtv', scores, new_values, precision=HIGHEST)
        last_log = cumulative[..., -1:]
        tail_decay = jnp.exp(last_log - cumulative)
        state = jnp.exp(last_log)[..., None] * state + jnp.einsum('shtk,shtv->shkv', key_block * tail_decay[..., None], new_values, precision=HIGHEST)
        return (state, block_out)
    zero_state = jnp.zeros((seq_count, head_count, key_size, value_size), jnp.float32)
    final_state, block_outs = lax.scan(block_step, zero_state, (to_blocks(queries), to_blocks(keys_now), to_blocks(values_now), to_blocks(beta_gate), to_blocks(decays)))
    block_outs = jnp.moveaxis(block_outs, (0, 2), (1, 3))
    return block_outs.reshape(seq_count, length, head_count, value_size)

def mixer_core(mixed_in, gate_in, conv_weight, a_log, dt_bias, out_gain):
    length = mixed_in.shape[1]
    key_size = DK
    qkv_width = 2 * DK + DV
    qkv_in = mixed_in[..., :qkv_width]
    padded = jnp.pad(qkv_in, ((0, 0), (CONV - 1, 0), (0, 0), (0, 0)))
    convolved = padded[:, 0:length] * conv_weight[0]
    for offset in range(1, CONV):
        convolved = convolved + padded[:, offset:offset + length] * conv_weight[offset]
    activated = jax.nn.silu(convolved)
    queries = unit_rows(activated[..., :key_size]) * key_size ** (-0.5)
    keys_now = unit_rows(activated[..., key_size:2 * key_size])
    values_now = activated[..., 2 * key_size:]
    beta_gate = jax.nn.sigmoid(gate_in[:, :, 1])
    decays = -jnp.exp(a_log) * jax.nn.softplus(gate_in[:, :, 0] + dt_bias)
    core_raw = delta_rule(queries, keys_now, values_now, beta_gate, decays)
    return rms_scale(core_raw, out_gain, 1e-05) * jax.nn.silu(mixed_in[..., qkv_width:])

def layer_block(inputs, cotangent, norm_gains, mix_weight, gate_weight, conv_weight, a_log, dt_bias, out_gain, out_weight, upgate_weight, down_weight):
    seq_count, length, model_width = inputs.shape
    row_count = seq_count * length
    head_count = mix_weight.shape[1]
    hidden_count = upgate_weight.shape[2]
    flat_in = inputs.reshape(row_count, model_width)
    normed_one = norm_apply(flat_in, norm_gains[0]).astype(jnp.bfloat16)
    flat_mix = mix_weight.reshape(model_width, -1)
    flat_gate = gate_weight.reshape(model_width, -1)
    mixed_in = jnp.dot(normed_one, flat_mix, preferred_element_type=jnp.float32).reshape(seq_count, length, head_count, -1)
    gate_in = jnp.dot(normed_one, flat_gate, preferred_element_type=jnp.float32).reshape(seq_count, length, 2, head_count)
    core_out, core_back = jax.vjp(mixer_core, mixed_in, gate_in, conv_weight, a_log, dt_bias, out_gain)
    core_half = core_out.reshape(row_count, -1).astype(jnp.bfloat16)
    flat_out = out_weight.reshape(-1, model_width)
    middle = flat_in + jnp.dot(core_half, flat_out, preferred_element_type=jnp.float32)
    normed_two = norm_apply(middle, norm_gains[1]).astype(jnp.bfloat16)
    flat_upgate = upgate_weight.reshape(model_width, -1)
    paired = jnp.dot(normed_two, flat_upgate, preferred_element_type=jnp.float32).reshape(row_count, 2, hidden_count)
    hidden_act, swiglu_back = jax.vjp(swiglu, paired)
    hidden_half = hidden_act.astype(jnp.bfloat16)
    outputs = middle + jnp.dot(hidden_half, down_weight, preferred_element_type=jnp.float32)
    cot_flat = cotangent.reshape(row_count, model_width)
    cot_half = cot_flat.astype(jnp.bfloat16)
    grad_down = jnp.dot(hidden_half.T, cot_half, preferred_element_type=jnp.float32)
    grad_hidden = jnp.dot(cot_half, down_weight.T, preferred_element_type=jnp.float32)
    grad_paired = swiglu_back(grad_hidden)[0].reshape(row_count, -1).astype(jnp.bfloat16)
    grad_upgate = jnp.dot(normed_two.T, grad_paired, preferred_element_type=jnp.float32).reshape(upgate_weight.shape)
    grad_normed_two = jnp.dot(grad_paired, flat_upgate.T, preferred_element_type=jnp.float32)
    norm_two_back = jax.vjp(norm_apply, middle, norm_gains[1])[1]
    grad_from_second, grad_gain_two = norm_two_back(grad_normed_two)
    grad_middle = cot_flat + grad_from_second
    middle_half = grad_middle.astype(jnp.bfloat16)
    grad_out = jnp.dot(core_half.T, middle_half, preferred_element_type=jnp.float32).reshape(out_weight.shape)
    grad_core = jnp.dot(middle_half, flat_out.T, preferred_element_type=jnp.float32).reshape(core_out.shape)
    grad_mixed, grad_gate_in, grad_conv, grad_a_log, grad_dt_bias, grad_out_gain = core_back(grad_core)
    mixed_grad_half = grad_mixed.reshape(row_count, -1).astype(jnp.bfloat16)
    gate_grad_half = grad_gate_in.reshape(row_count, -1).astype(jnp.bfloat16)
    grad_mix = jnp.dot(normed_one.T, mixed_grad_half, preferred_element_type=jnp.float32).reshape(mix_weight.shape)
    grad_gate = jnp.dot(normed_one.T, gate_grad_half, preferred_element_type=jnp.float32).reshape(gate_weight.shape)
    grad_normed_one = jnp.dot(mixed_grad_half, flat_mix.T, preferred_element_type=jnp.float32) + jnp.dot(gate_grad_half, flat_gate.T, preferred_element_type=jnp.float32)
    norm_one_back = jax.vjp(norm_apply, flat_in, norm_gains[0])[1]
    grad_from_first, grad_gain_one = norm_one_back(grad_normed_one)
    grad_inputs = grad_middle + grad_from_first
    gradients = (jnp.stack([grad_gain_one, grad_gain_two]), grad_mix, grad_gate, grad_conv, grad_a_log, grad_dt_bias, grad_out_gain, grad_out, grad_upgate, grad_down)
    return (outputs.reshape(inputs.shape), grad_inputs.reshape(inputs.shape), gradients)

def clip_gradient(gradient):
    limit = CLIP_SHARE * math.sqrt(gradient.size)
    scale = jnp.minimum(1.0, limit * lax.rsqrt(jnp.sum(gradient * gradient) + 1e-12))
    return gradient * scale

def adamw_update(weight, gradient, moment, second, rate):
    clipped = clip_gradient(gradient)
    new_moment = 0.9 * moment + 0.1 * clipped
    new_second = 0.95 * second + 0.05 * clipped * clipped
    first_fix = 1.0 - 0.9 ** STEP
    second_fix = 1.0 - 0.95 ** STEP
    update = new_moment / first_fix / (jnp.sqrt(new_second / second_fix) + 1e-08) + 0.1 * weight
    return (weight - rate * update, new_moment, new_second)

def reference(inputs, cotangent, norm_gains, mix_weight, gate_weight, conv_weight, a_log, dt_bias, out_gain, out_weight, upgate_weight, down_weight, moment_norm_gains, moment_mix_weight, moment_gate_weight, moment_conv_weight, moment_a_log, moment_dt_bias, moment_out_gain, moment_out_weight, moment_upgate_weight, moment_down_weight, second_norm_gains, second_mix_weight, second_gate_weight, second_conv_weight, second_a_log, second_dt_bias, second_out_gain, second_out_weight, second_upgate_weight, second_down_weight):
    parameters = (norm_gains, mix_weight, gate_weight, conv_weight, a_log, dt_bias, out_gain, out_weight, upgate_weight, down_weight)
    mix_half = mix_weight.astype(jnp.bfloat16)
    gate_half = gate_weight.astype(jnp.bfloat16)
    out_half = out_weight.astype(jnp.bfloat16)
    upgate_half = upgate_weight.astype(jnp.bfloat16)
    down_half = down_weight.astype(jnp.bfloat16)
    group_size = 8
    total_seqs = inputs.shape[0] // LEN
    shaped_in = inputs.reshape(total_seqs // group_size, group_size, LEN, D)
    shaped_cot = cotangent.reshape(total_seqs // group_size, group_size, LEN, D)

    def scan_step(totals, block_items):
        block_out, block_grad, gradients = layer_block(block_items[0], block_items[1], norm_gains, mix_half, gate_half, conv_weight, a_log, dt_bias, out_gain, out_half, upgate_half, down_half)
        totals = jax.tree.map(jnp.add, totals, gradients)
        return (totals, (block_out, block_grad))
    zero_grads = tuple((jnp.zeros(parameter.shape, jnp.float32) for parameter in parameters))
    grads, stacked = lax.scan(scan_step, zero_grads, (shaped_in, shaped_cot))
    outputs = stacked[0].reshape(inputs.shape)
    grad_inputs = stacked[1].reshape(inputs.shape)
    grad_norm_gains, grad_mix_weight, grad_gate_weight, grad_conv_weight, grad_a_log, grad_dt_bias, grad_out_gain, grad_out_weight, grad_upgate_weight, grad_down_weight = grads
    new_norm_gains, new_moment_norm_gains, new_second_norm_gains = adamw_update(norm_gains, grad_norm_gains, moment_norm_gains, second_norm_gains, RATE_VECTOR)
    new_mix_weight, new_moment_mix_weight, new_second_mix_weight = adamw_update(mix_weight, grad_mix_weight, moment_mix_weight, second_mix_weight, RATE_MATRIX)
    new_gate_weight, new_moment_gate_weight, new_second_gate_weight = adamw_update(gate_weight, grad_gate_weight, moment_gate_weight, second_gate_weight, RATE_MATRIX)
    new_conv_weight, new_moment_conv_weight, new_second_conv_weight = adamw_update(conv_weight, grad_conv_weight, moment_conv_weight, second_conv_weight, RATE_VECTOR)
    new_a_log, new_moment_a_log, new_second_a_log = adamw_update(a_log, grad_a_log, moment_a_log, second_a_log, RATE_VECTOR)
    new_dt_bias, new_moment_dt_bias, new_second_dt_bias = adamw_update(dt_bias, grad_dt_bias, moment_dt_bias, second_dt_bias, RATE_VECTOR)
    new_out_gain, new_moment_out_gain, new_second_out_gain = adamw_update(out_gain, grad_out_gain, moment_out_gain, second_out_gain, RATE_VECTOR)
    new_out_weight, new_moment_out_weight, new_second_out_weight = adamw_update(out_weight, grad_out_weight, moment_out_weight, second_out_weight, RATE_MATRIX)
    new_upgate_weight, new_moment_upgate_weight, new_second_upgate_weight = adamw_update(upgate_weight, grad_upgate_weight, moment_upgate_weight, second_upgate_weight, RATE_MATRIX)
    new_down_weight, new_moment_down_weight, new_second_down_weight = adamw_update(down_weight, grad_down_weight, moment_down_weight, second_down_weight, RATE_MATRIX)
    return (outputs, grad_inputs, grad_norm_gains, grad_mix_weight, grad_gate_weight, grad_conv_weight, grad_a_log, grad_dt_bias, grad_out_gain, grad_out_weight, grad_upgate_weight, grad_down_weight, new_norm_gains, new_mix_weight, new_gate_weight, new_conv_weight, new_a_log, new_dt_bias, new_out_gain, new_out_weight, new_upgate_weight, new_down_weight, new_moment_norm_gains, new_moment_mix_weight, new_moment_gate_weight, new_moment_conv_weight, new_moment_a_log, new_moment_dt_bias, new_moment_out_gain, new_moment_out_weight, new_moment_upgate_weight, new_moment_down_weight, new_second_norm_gains, new_second_mix_weight, new_second_gate_weight, new_second_conv_weight, new_second_a_log, new_second_dt_bias, new_second_out_gain, new_second_out_weight, new_second_upgate_weight, new_second_down_weight)
```

```python
import math

import jax
import jax.numpy as jnp
from jax import lax
from jax.sharding import PartitionSpec as P

DK = 128
DV = 256
CONV = 4
SPAN = 64
LEN = 384
STEP = 3


HIGHEST = lax.Precision.HIGHEST
RATE_MATRIX = 0.01
RATE_VECTOR = 0.1
CLIP_SHARE = 0.3


def rms_scale(rows_in, gain_row, epsilon):
    return (
        rows_in
        * lax.rsqrt(jnp.mean(rows_in * rows_in, axis=-1, keepdims=True) + epsilon)
        * gain_row
    )


def norm_apply(rows_in, gain_row):
    return rms_scale(rows_in, gain_row, 1e-05)


def unit_rows(rows_in):
    return rows_in * lax.rsqrt(jnp.sum(rows_in * rows_in, axis=-1, keepdims=True) + 1e-06)


def swiglu(paired):
    return jax.nn.silu(paired[:, 0]) * paired[:, 1]


HIGH = lax.Precision.HIGH


def unit_lower_product(lower_part):
    size_now = lower_part.shape[-1]
    identity = jnp.eye(size_now, dtype=jnp.float32)
    inverse = identity - lower_part
    power_now = jnp.matmul(lower_part, lower_part, precision=HIGHEST)
    steps = size_now.bit_length() - 2
    for repeat in range(steps):
        inverse = inverse + jnp.matmul(inverse, power_now, precision=HIGHEST)
        if repeat + 1 < steps:
            power_now = jnp.matmul(power_now, power_now, precision=HIGHEST)
    return inverse


@jax.custom_vjp
def inverse_unit_lower(lower_part):
    return unit_lower_product(lower_part)


def inverse_forward(lower_part):
    inverse = unit_lower_product(lower_part)
    return inverse, inverse


def inverse_backward(inverse, grad_inverse):
    flipped = jnp.swapaxes(inverse, -1, -2)
    inner = jnp.matmul(flipped, grad_inverse, precision=HIGH)
    return (-jnp.matmul(inner, flipped, precision=HIGH),)


inverse_unit_lower.defvjp(inverse_forward, inverse_backward)


def run_states(steps_in, adds_in):
    block_count = steps_in.shape[2]
    state = jnp.zeros_like(adds_in[:, :, 0])
    states = [state]
    for index in range(block_count - 1):
        state = adds_in[:, :, index] + jnp.matmul(steps_in[:, :, index], state, precision=HIGH)
        states.append(state)
    return jnp.stack(states, axis=2)


@jax.custom_vjp
def chain_states(steps_in, adds_in):
    return run_states(steps_in, adds_in)


def chain_forward(steps_in, adds_in):
    states = run_states(steps_in, adds_in)
    return states, (steps_in, states)


def chain_backward(kept, grad_states):
    steps_in, states = kept
    block_count = steps_in.shape[2]
    grad_now = jnp.zeros_like(grad_states[:, :, 0])
    grads = [grad_now]
    for index in range(block_count - 1, 0, -1):
        if index == block_count - 1:
            grad_now = grad_states[:, :, index]
        else:
            grad_now = grad_states[:, :, index] + jnp.einsum(
                "shkj,shkv->shjv", steps_in[:, :, index], grad_now, precision=HIGH
            )
        grads.append(grad_now)
    grad_adds = jnp.stack(grads[::-1], axis=2)
    grad_steps = jnp.einsum("shnkv,shnjv->shnkj", grad_adds, states, precision=HIGH)
    return grad_steps, grad_adds


chain_states.defvjp(chain_forward, chain_backward)


def delta_rule(queries, keys_now, values_now, beta_gate, decays):
    seq_count, head_count, length, key_size = keys_now.shape
    block_count = length // SPAN

    def to_blocks(array_in):
        return array_in.reshape((seq_count, head_count, block_count, SPAN) + array_in.shape[3:])

    strict = jnp.tril(jnp.ones((SPAN, SPAN), bool), -1)
    inclusive = jnp.tril(jnp.ones((SPAN, SPAN), bool))
    queries, keys_now, values_now, beta_gate, decays = (
        to_blocks(queries),
        to_blocks(keys_now),
        to_blocks(values_now),
        to_blocks(beta_gate),
        to_blocks(decays),
    )
    cumulative = jnp.einsum(
        "shnu,tu->shnt", decays, inclusive.astype(jnp.float32), precision=HIGHEST
    )
    log_gaps = cumulative[..., :, None] - cumulative[..., None, :]
    fall_inclusive = jnp.where(inclusive, jnp.exp(jnp.where(inclusive, log_gaps, 0.0)), 0.0)
    fall_strict = jnp.where(strict, fall_inclusive, 0.0)
    both = jnp.concatenate([keys_now, queries], axis=3)
    products = jnp.einsum("shntk,shnuk->shntu", both, keys_now, precision=HIGH)
    lower_part = beta_gate[..., None] * products[..., :SPAN, :] * fall_strict
    scores = products[..., SPAN:, :] * fall_inclusive
    inverse = inverse_unit_lower(lower_part)
    growth = jnp.exp(cumulative)
    sides = jnp.concatenate(
        [(beta_gate * growth)[..., None] * keys_now, beta_gate[..., None] * values_now], axis=-1
    )
    solved = jnp.einsum("shntu,shnuw->shntw", inverse, sides, precision=HIGH)
    last_log = cumulative[..., -1:]
    tail_keys = keys_now * jnp.exp(last_log - cumulative)[..., None]
    joined = jnp.einsum("shntk,shntw->shnkw", tail_keys, solved, precision=HIGH)
    identity = jnp.eye(key_size, dtype=jnp.float32)
    steps_in = jnp.exp(last_log)[..., None] * identity - joined[..., :key_size]
    states = chain_states(steps_in, joined[..., key_size:])
    readers = jnp.concatenate([solved[..., :key_size], growth[..., None] * queries], axis=3)
    read = jnp.einsum("shntk,shnkv->shntv", readers, states, precision=HIGH)
    new_values = solved[..., key_size:] - read[..., :SPAN, :]
    block_outs = read[..., SPAN:, :] + jnp.einsum(
        "shntu,shnuv->shntv", scores, new_values, precision=HIGH
    )
    return block_outs.reshape(values_now.shape[:2] + (length, values_now.shape[-1]))


def mixer_core(mixed_in, gate_in, conv_weight, a_log, dt_bias, out_gain):
    length = mixed_in.shape[2]
    key_size = DK
    qkv_width = 2 * DK + DV
    qkv_in = mixed_in[..., :qkv_width]
    padded = jnp.pad(qkv_in, ((0, 0), (0, 0), (CONV - 1, 0), (0, 0)))
    convolved = padded[:, :, 0:length] * conv_weight[0][:, None]
    for offset in range(1, CONV):
        convolved = convolved + padded[:, :, offset : offset + length] * conv_weight[offset][:, None]
    activated = jax.nn.silu(convolved)
    queries = unit_rows(activated[..., :key_size]) * key_size ** (-0.5)
    keys_now = unit_rows(activated[..., key_size : 2 * key_size])
    values_now = activated[..., 2 * key_size :]
    beta_gate = jax.nn.sigmoid(gate_in[:, 1])
    decays = -jnp.exp(a_log)[:, None] * jax.nn.softplus(gate_in[:, 0] + dt_bias[:, None])
    core_raw = delta_rule(queries, keys_now, values_now, beta_gate, decays)
    return rms_scale(core_raw, out_gain, 1e-05) * jax.nn.silu(mixed_in[..., qkv_width:])


def adamw_update(weight, gradient, moment, second, rate, squares, entries):
    limit = CLIP_SHARE * math.sqrt(entries)
    scale = jnp.minimum(1.0, limit * lax.rsqrt(squares + 1e-12))
    clipped = gradient * scale
    new_moment = 0.9 * moment + 0.1 * clipped
    new_second = 0.95 * second + 0.05 * clipped * clipped
    first_fix = 1.0 - 0.9**STEP
    second_fix = 1.0 - 0.95**STEP
    update = new_moment / first_fix / (jnp.sqrt(new_second / second_fix) + 1e-08) + 0.1 * weight
    return (weight - rate * update, new_moment, new_second)


def square_sum(values):
    return jnp.sum(values * values)


def gathered_total(flat_value, axis_names):
    columns = -(-flat_value.size // 1024) * 128
    block = jnp.pad(flat_value, (0, 8 * columns - flat_value.size)).reshape(8, columns)
    blocks = lax.all_gather(block, axis_names, axis=0, tiled=True)
    return jnp.sum(blocks.reshape(-1, 8, columns), axis=0).reshape(-1)


def tensor_total(partial_value):
    return lax.psum(partial_value, "tensor")


def body(
    inputs,
    cotangent,
    norm_gains,
    mix_weight,
    gate_weight,
    conv_weight,
    a_log,
    dt_bias,
    out_gain,
    out_weight,
    upgate_weight,
    down_weight,
    moment_norm_gains,
    moment_mix_weight,
    moment_gate_weight,
    moment_conv_weight,
    moment_a_log,
    moment_dt_bias,
    moment_out_gain,
    moment_out_weight,
    moment_upgate_weight,
    moment_down_weight,
    second_norm_gains,
    second_mix_weight,
    second_gate_weight,
    second_conv_weight,
    second_a_log,
    second_dt_bias,
    second_out_gain,
    second_out_weight,
    second_upgate_weight,
    second_down_weight,
):
    owned_rows = mix_weight.shape[0]
    head_count = mix_weight.shape[1]
    hidden_count = upgate_weight.shape[2]
    mix_columns = mix_weight.size // owned_rows
    gate_columns = gate_weight.size // owned_rows
    joint_shard = jnp.concatenate(
        [
            mix_weight.astype(jnp.bfloat16).reshape(owned_rows, -1),
            gate_weight.astype(jnp.bfloat16).reshape(owned_rows, -1),
            jnp.zeros((owned_rows, 128 - gate_columns), jnp.bfloat16),
        ],
        axis=1,
    )
    joint_full = lax.all_gather(joint_shard, "dp", axis=0, tiled=True)
    out_full = lax.all_gather(out_weight.astype(jnp.bfloat16), "dp", axis=2, tiled=True)
    upgate_full = lax.all_gather(
        upgate_weight.astype(jnp.bfloat16), "dp", axis=0, tiled=True
    )
    down_full = lax.all_gather(down_weight.astype(jnp.bfloat16), "dp", axis=1, tiled=True)
    row_count, model_width = inputs.shape
    seq_count = row_count // LEN
    normed_one = norm_apply(inputs, norm_gains[0]).astype(jnp.bfloat16)
    joint_in = jnp.dot(normed_one, joint_full, preferred_element_type=jnp.float32)
    mixed_in = jnp.swapaxes(
        joint_in[:, :mix_columns].reshape(seq_count, LEN, head_count, -1), 1, 2
    )
    gate_in = jnp.moveaxis(
        joint_in[:, mix_columns : mix_columns + gate_columns].reshape(
            seq_count, LEN, 2, head_count
        ),
        1,
        3,
    )
    core_out, core_back = jax.vjp(
        mixer_core, mixed_in, gate_in, conv_weight, a_log, dt_bias, out_gain
    )
    core_half = (
        jnp.swapaxes(core_out.astype(jnp.bfloat16), 1, 2).reshape(row_count, -1)
    )
    flat_out = out_full.reshape(-1, model_width)
    middle_part = jnp.dot(core_half, flat_out, preferred_element_type=jnp.float32).astype(
        jnp.bfloat16
    )
    middle_part, upgate_full, down_full = lax.optimization_barrier(
        (middle_part, upgate_full, down_full)
    )
    middle = inputs + tensor_total(middle_part).astype(jnp.float32)
    normed_rows = norm_apply(middle, norm_gains[1]).astype(jnp.bfloat16)
    flat_upgate = upgate_full.reshape(model_width, -1)
    paired = jnp.dot(normed_rows, flat_upgate, preferred_element_type=jnp.float32).reshape(
        row_count, 2, hidden_count
    )
    hidden_act, swiglu_back = jax.vjp(swiglu, paired)
    hidden_half = hidden_act.astype(jnp.bfloat16)
    cot_half = cotangent.astype(jnp.bfloat16)
    grad_hidden = jnp.dot(cot_half, down_full.T, preferred_element_type=jnp.float32)
    grad_paired = swiglu_back(grad_hidden)[0].reshape(row_count, -1).astype(jnp.bfloat16)
    grad_normed_two = tensor_total(
        jnp.dot(grad_paired, flat_upgate.T, preferred_element_type=jnp.float32).astype(
            jnp.bfloat16
        )
    )
    output_part = jnp.dot(hidden_half, down_full, preferred_element_type=jnp.float32).astype(
        jnp.bfloat16
    )
    grad_down = jnp.dot(
        hidden_half.T, cot_half, preferred_element_type=jnp.float32
    ).astype(jnp.bfloat16)
    grad_upgate = (
        jnp.dot(normed_rows.T, grad_paired, preferred_element_type=jnp.float32)
        .astype(jnp.bfloat16)
        .reshape(upgate_full.shape)
    )
    grad_normed_two, output_part, grad_down, grad_upgate = lax.optimization_barrier(
        (grad_normed_two, output_part, grad_down, grad_upgate)
    )
    grad_normed_two = grad_normed_two.astype(jnp.float32)
    shard_upgate = lax.psum_scatter(grad_upgate, "dp", scatter_dimension=0, tiled=True)
    shard_down = lax.psum_scatter(grad_down, "dp", scatter_dimension=1, tiled=True)
    output_total = tensor_total(output_part)
    norm_two_back = jax.vjp(norm_apply, middle, norm_gains[1])[1]
    grad_from_second, grad_gain_two = norm_two_back(grad_normed_two)
    grad_middle = cotangent + grad_from_second
    middle_rows = grad_middle.astype(jnp.bfloat16)
    grad_out = jnp.dot(core_half.T, middle_rows, preferred_element_type=jnp.float32).reshape(
        out_full.shape
    )
    shard_out = lax.psum_scatter(
        grad_out.astype(jnp.bfloat16), "dp", scatter_dimension=2, tiled=True
    )
    grad_core = jnp.swapaxes(
        jnp.dot(middle_rows, flat_out.T, preferred_element_type=jnp.float32).reshape(
            seq_count, LEN, head_count, -1
        ),
        1,
        2,
    )
    grad_mixed, grad_gate_in, grad_conv, grad_a_log_part, grad_dt_part, grad_gain_part = core_back(
        grad_core
    )
    joint_grad_half = jnp.concatenate(
        [
            jnp.swapaxes(grad_mixed.astype(jnp.bfloat16), 1, 2).reshape(row_count, -1),
            jnp.moveaxis(grad_gate_in.astype(jnp.bfloat16), 3, 1).reshape(row_count, -1),
            jnp.zeros((row_count, 128 - gate_columns), jnp.bfloat16),
        ],
        axis=1,
    )
    partial_first = jnp.dot(
        joint_grad_half, joint_full.T, preferred_element_type=jnp.float32
    ).astype(jnp.bfloat16)
    partial_first, output_total, shard_upgate, shard_down, shard_out = lax.optimization_barrier(
        (partial_first, output_total, shard_upgate, shard_down, shard_out)
    )
    output_rows = middle + output_total.astype(jnp.float32)
    shard_upgate, shard_down, shard_out = (
        shard_upgate.astype(jnp.float32),
        shard_down.astype(jnp.float32),
        shard_out.astype(jnp.float32),
    )
    grad_normed_one = lax.psum(partial_first, "tensor").astype(jnp.float32)
    grad_joint = jnp.dot(normed_one.T, joint_grad_half, preferred_element_type=jnp.float32)
    shard_joint = lax.psum_scatter(
        grad_joint.astype(jnp.bfloat16), "dp", scatter_dimension=0, tiled=True
    ).astype(jnp.float32)
    shard_mix = shard_joint[:, :mix_columns].reshape(mix_weight.shape)
    shard_gate = shard_joint[:, mix_columns : mix_columns + gate_columns].reshape(
        gate_weight.shape
    )
    norm_one_back = jax.vjp(norm_apply, inputs, norm_gains[0])[1]
    grad_from_first, grad_gain_one = norm_one_back(grad_normed_one)
    grad_input_rows = grad_middle + grad_from_first
    dp_count = lax.axis_size("dp")
    tensor_count = lax.axis_size("tensor")
    early = jnp.concatenate(
        [
            grad_conv.reshape(-1),
            grad_gain_two.reshape(-1),
            grad_a_log_part.reshape(-1),
            grad_dt_part.reshape(-1),
        ]
    )
    early = gathered_total(early, "dp")
    cut = [grad_conv.size, model_width, a_log.size, dt_bias.size]
    grad_conv_weight = early[: cut[0]].reshape(conv_weight.shape)
    grad_gain_two = early[cut[0] : cut[0] + cut[1]]
    grad_a_log = early[cut[0] + cut[1] : cut[0] + cut[1] + cut[2]]
    grad_dt_bias = early[cut[0] + cut[1] + cut[2] : sum(cut)]
    local_squares = jnp.stack(
        [
            square_sum(shard_mix),
            square_sum(shard_gate),
            square_sum(shard_out),
            square_sum(shard_upgate),
            square_sum(shard_down),
            square_sum(grad_conv_weight) / dp_count,
            square_sum(grad_a_log) / dp_count,
            square_sum(grad_dt_bias) / dp_count,
        ]
    )
    late = jnp.concatenate([grad_gain_one / tensor_count, grad_gain_part, local_squares])
    late = gathered_total(late, ("tensor", "dp"))
    grad_norm_gains = jnp.stack([late[:model_width], grad_gain_two])
    grad_out_gain = late[model_width : model_width + out_gain.size]
    total_squares = late[model_width + out_gain.size : model_width + out_gain.size + 8]
    spread = dp_count * tensor_count
    new_norm_gains, new_moment_norm_gains, new_second_norm_gains = adamw_update(
        norm_gains,
        grad_norm_gains,
        moment_norm_gains,
        second_norm_gains,
        RATE_VECTOR,
        square_sum(grad_norm_gains),
        grad_norm_gains.size,
    )
    new_mix_weight, new_moment_mix_weight, new_second_mix_weight = adamw_update(
        mix_weight,
        shard_mix,
        moment_mix_weight,
        second_mix_weight,
        RATE_MATRIX,
        total_squares[0],
        shard_mix.size * spread,
    )
    new_gate_weight, new_moment_gate_weight, new_second_gate_weight = adamw_update(
        gate_weight,
        shard_gate,
        moment_gate_weight,
        second_gate_weight,
        RATE_MATRIX,
        total_squares[1],
        shard_gate.size * spread,
    )
    new_conv_weight, new_moment_conv_weight, new_second_conv_weight = adamw_update(
        conv_weight,
        grad_conv_weight,
        moment_conv_weight,
        second_conv_weight,
        RATE_VECTOR,
        total_squares[5],
        grad_conv_weight.size * tensor_count,
    )
    new_a_log, new_moment_a_log, new_second_a_log = adamw_update(
        a_log,
        grad_a_log,
        moment_a_log,
        second_a_log,
        RATE_VECTOR,
        total_squares[6],
        grad_a_log.size * tensor_count,
    )
    new_dt_bias, new_moment_dt_bias, new_second_dt_bias = adamw_update(
        dt_bias,
        grad_dt_bias,
        moment_dt_bias,
        second_dt_bias,
        RATE_VECTOR,
        total_squares[7],
        grad_dt_bias.size * tensor_count,
    )
    new_out_gain, new_moment_out_gain, new_second_out_gain = adamw_update(
        out_gain,
        grad_out_gain,
        moment_out_gain,
        second_out_gain,
        RATE_VECTOR,
        square_sum(grad_out_gain),
        grad_out_gain.size,
    )
    new_out_weight, new_moment_out_weight, new_second_out_weight = adamw_update(
        out_weight,
        shard_out,
        moment_out_weight,
        second_out_weight,
        RATE_MATRIX,
        total_squares[2],
        shard_out.size * spread,
    )
    new_upgate_weight, new_moment_upgate_weight, new_second_upgate_weight = adamw_update(
        upgate_weight,
        shard_upgate,
        moment_upgate_weight,
        second_upgate_weight,
        RATE_MATRIX,
        total_squares[3],
        shard_upgate.size * spread,
    )
    new_down_weight, new_moment_down_weight, new_second_down_weight = adamw_update(
        down_weight,
        shard_down,
        moment_down_weight,
        second_down_weight,
        RATE_MATRIX,
        total_squares[4],
        shard_down.size * spread,
    )
    return (
        output_rows,
        grad_input_rows,
        grad_norm_gains,
        shard_mix,
        shard_gate,
        grad_conv_weight,
        grad_a_log,
        grad_dt_bias,
        grad_out_gain,
        shard_out,
        shard_upgate,
        shard_down,
        new_norm_gains,
        new_mix_weight,
        new_gate_weight,
        new_conv_weight,
        new_a_log,
        new_dt_bias,
        new_out_gain,
        new_out_weight,
        new_upgate_weight,
        new_down_weight,
        new_moment_norm_gains,
        new_moment_mix_weight,
        new_moment_gate_weight,
        new_moment_conv_weight,
        new_moment_a_log,
        new_moment_dt_bias,
        new_moment_out_gain,
        new_moment_out_weight,
        new_moment_upgate_weight,
        new_moment_down_weight,
        new_second_norm_gains,
        new_second_mix_weight,
        new_second_gate_weight,
        new_second_conv_weight,
        new_second_a_log,
        new_second_dt_bias,
        new_second_out_gain,
        new_second_out_weight,
        new_second_upgate_weight,
        new_second_down_weight,
    )


def solution(mesh):
    placed = (
        P("dp", None),
        P("dp", None),
        P(),
        P("dp", "tensor", None),
        P("dp", None, "tensor"),
        P(None, "tensor", None),
        P("tensor"),
        P("tensor"),
        P(),
        P("tensor", None, "dp"),
        P("dp", None, "tensor"),
        P("tensor", "dp"),
        P(),
        P("dp", "tensor", None),
        P("dp", None, "tensor"),
        P(None, "tensor", None),
        P("tensor"),
        P("tensor"),
        P(),
        P("tensor", None, "dp"),
        P("dp", None, "tensor"),
        P("tensor", "dp"),
        P(),
        P("dp", "tensor", None),
        P("dp", None, "tensor"),
        P(None, "tensor", None),
        P("tensor"),
        P("tensor"),
        P(),
        P("tensor", None, "dp"),
        P("dp", None, "tensor"),
        P("tensor", "dp"),
    )
    return jax.shard_map(
        body,
        mesh=mesh,
        in_specs=placed,
        out_specs=(
            P("dp", None),
            P("dp", None),
            P(),
            P("dp", "tensor", None),
            P("dp", None, "tensor"),
            P(None, "tensor", None),
            P("tensor"),
            P("tensor"),
            P(),
            P("tensor", None, "dp"),
            P("dp", None, "tensor"),
            P("tensor", "dp"),
            P(),
            P("dp", "tensor", None),
            P("dp", None, "tensor"),
            P(None, "tensor", None),
            P("tensor"),
            P("tensor"),
            P(),
            P("tensor", None, "dp"),
            P("dp", None, "tensor"),
            P("tensor", "dp"),
            P(),
            P("dp", "tensor", None),
            P("dp", None, "tensor"),
            P(None, "tensor", None),
            P("tensor"),
            P("tensor"),
            P(),
            P("tensor", None, "dp"),
            P("dp", None, "tensor"),
            P("tensor", "dp"),
            P(),
            P("dp", "tensor", None),
            P("dp", None, "tensor"),
            P(None, "tensor", None),
            P("tensor"),
            P("tensor"),
            P(),
            P("tensor", None, "dp"),
            P("dp", None, "tensor"),
            P("tensor", "dp"),
        ),
        check_vma=False,
    )
```

```python
import math

import jax
import jax.numpy as jnp
from jax import lax
from jax.sharding import PartitionSpec as P

DK = 128
DV = 256
CONV = 4
SPAN = 64
LEN = 384
STEP = 3


HIGHEST = lax.Precision.HIGHEST
RATE_MATRIX = 0.01
RATE_VECTOR = 0.1
CLIP_SHARE = 0.3


def rms_scale(rows_in, gain_row, epsilon):
    return (
        rows_in
        * lax.rsqrt(jnp.mean(rows_in * rows_in, axis=-1, keepdims=True) + epsilon)
        * gain_row
    )


def norm_apply(rows_in, gain_row):
    return rms_scale(rows_in, gain_row, 1e-05)


def unit_rows(rows_in):
    return rows_in * lax.rsqrt(jnp.sum(rows_in * rows_in, axis=-1, keepdims=True) + 1e-06)


def swiglu(paired):
    return jax.nn.silu(paired[:, 0]) * paired[:, 1]


HIGH = lax.Precision.HIGH


def unit_lower_product(lower_part):
    size_now = lower_part.shape[-1]
    identity = jnp.eye(size_now, dtype=jnp.float32)
    inverse = identity - lower_part
    power_now = jnp.matmul(lower_part, lower_part, precision=HIGHEST)
    steps = size_now.bit_length() - 2
    for repeat in range(steps):
        inverse = inverse + jnp.matmul(inverse, power_now, precision=HIGHEST)
        if repeat + 1 < steps:
            power_now = jnp.matmul(power_now, power_now, precision=HIGHEST)
    return inverse


@jax.custom_vjp
def inverse_unit_lower(lower_part):
    return unit_lower_product(lower_part)


def inverse_forward(lower_part):
    inverse = unit_lower_product(lower_part)
    return inverse, inverse


def inverse_backward(inverse, grad_inverse):
    flipped = jnp.swapaxes(inverse, -1, -2)
    inner = jnp.matmul(flipped, grad_inverse, precision=HIGH)
    return (-jnp.matmul(inner, flipped, precision=HIGH),)


inverse_unit_lower.defvjp(inverse_forward, inverse_backward)


def run_states(steps_in, adds_in):
    block_count = steps_in.shape[2]
    state = jnp.zeros_like(adds_in[:, :, 0])
    states = [state]
    for index in range(block_count - 1):
        state = adds_in[:, :, index] + jnp.matmul(steps_in[:, :, index], state, precision=HIGH)
        states.append(state)
    return jnp.stack(states, axis=2)


@jax.custom_vjp
def chain_states(steps_in, adds_in):
    return run_states(steps_in, adds_in)


def chain_forward(steps_in, adds_in):
    states = run_states(steps_in, adds_in)
    return states, (steps_in, states)


def chain_backward(kept, grad_states):
    steps_in, states = kept
    block_count = steps_in.shape[2]
    grad_now = jnp.zeros_like(grad_states[:, :, 0])
    grads = [grad_now]
    for index in range(block_count - 1, 0, -1):
        if index == block_count - 1:
            grad_now = grad_states[:, :, index]
        else:
            grad_now = grad_states[:, :, index] + jnp.einsum(
                "shkj,shkv->shjv", steps_in[:, :, index], grad_now, precision=HIGH
            )
        grads.append(grad_now)
    grad_adds = jnp.stack(grads[::-1], axis=2)
    grad_steps = jnp.einsum("shnkv,shnjv->shnkj", grad_adds, states, precision=HIGH)
    return grad_steps, grad_adds


chain_states.defvjp(chain_forward, chain_backward)


def delta_rule(queries, keys_now, values_now, beta_gate, decays):
    seq_count, head_count, length, key_size = keys_now.shape
    block_count = length // SPAN

    def to_blocks(array_in):
        return array_in.reshape((seq_count, head_count, block_count, SPAN) + array_in.shape[3:])

    strict = jnp.tril(jnp.ones((SPAN, SPAN), bool), -1)
    inclusive = jnp.tril(jnp.ones((SPAN, SPAN), bool))
    queries, keys_now, values_now, beta_gate, decays = (
        to_blocks(queries),
        to_blocks(keys_now),
        to_blocks(values_now),
        to_blocks(beta_gate),
        to_blocks(decays),
    )
    cumulative = jnp.einsum(
        "shnu,tu->shnt", decays, inclusive.astype(jnp.float32), precision=HIGHEST
    )
    log_gaps = cumulative[..., :, None] - cumulative[..., None, :]
    fall_inclusive = jnp.where(inclusive, jnp.exp(jnp.where(inclusive, log_gaps, 0.0)), 0.0)
    fall_strict = jnp.where(strict, fall_inclusive, 0.0)
    both = jnp.concatenate([keys_now, queries], axis=3)
    products = jnp.einsum("shntk,shnuk->shntu", both, keys_now, precision=HIGH)
    lower_part = beta_gate[..., None] * products[..., :SPAN, :] * fall_strict
    scores = products[..., SPAN:, :] * fall_inclusive
    inverse = inverse_unit_lower(lower_part)
    growth = jnp.exp(cumulative)
    sides = jnp.concatenate(
        [(beta_gate * growth)[..., None] * keys_now, beta_gate[..., None] * values_now], axis=-1
    )
    solved = jnp.einsum("shntu,shnuw->shntw", inverse, sides, precision=HIGH)
    last_log = cumulative[..., -1:]
    tail_keys = keys_now * jnp.exp(last_log - cumulative)[..., None]
    joined = jnp.einsum("shntk,shntw->shnkw", tail_keys, solved, precision=HIGH)
    identity = jnp.eye(key_size, dtype=jnp.float32)
    steps_in = jnp.exp(last_log)[..., None] * identity - joined[..., :key_size]
    states = chain_states(steps_in, joined[..., key_size:])
    readers = jnp.concatenate([solved[..., :key_size], growth[..., None] * queries], axis=3)
    read = jnp.einsum("shntk,shnkv->shntv", readers, states, precision=HIGH)
    new_values = solved[..., key_size:] - read[..., :SPAN, :]
    block_outs = read[..., SPAN:, :] + jnp.einsum(
        "shntu,shnuv->shntv", scores, new_values, precision=HIGH
    )
    return block_outs.reshape(values_now.shape[:2] + (length, values_now.shape[-1]))


def mixer_core(mixed_in, gate_in, conv_weight, a_log, dt_bias, out_gain):
    length = mixed_in.shape[2]
    key_size = DK
    qkv_width = 2 * DK + DV
    qkv_in = mixed_in[..., :qkv_width]
    padded = jnp.pad(qkv_in, ((0, 0), (0, 0), (CONV - 1, 0), (0, 0)))
    convolved = padded[:, :, 0:length] * conv_weight[0][:, None]
    for offset in range(1, CONV):
        convolved = convolved + padded[:, :, offset : offset + length] * conv_weight[offset][:, None]
    activated = jax.nn.silu(convolved)
    queries = unit_rows(activated[..., :key_size]) * key_size ** (-0.5)
    keys_now = unit_rows(activated[..., key_size : 2 * key_size])
    values_now = activated[..., 2 * key_size :]
    beta_gate = jax.nn.sigmoid(gate_in[:, 1])
    decays = -jnp.exp(a_log)[:, None] * jax.nn.softplus(gate_in[:, 0] + dt_bias[:, None])
    core_raw = delta_rule(queries, keys_now, values_now, beta_gate, decays)
    return rms_scale(core_raw, out_gain, 1e-05) * jax.nn.silu(mixed_in[..., qkv_width:])


def adamw_update(weight, gradient, moment, second, rate, squares, entries):
    limit = CLIP_SHARE * math.sqrt(entries)
    scale = jnp.minimum(1.0, limit * lax.rsqrt(squares + 1e-12))
    clipped = gradient * scale
    new_moment = 0.9 * moment + 0.1 * clipped
    new_second = 0.95 * second + 0.05 * clipped * clipped
    first_fix = 1.0 - 0.9**STEP
    second_fix = 1.0 - 0.95**STEP
    update = new_moment / first_fix / (jnp.sqrt(new_second / second_fix) + 1e-08) + 0.1 * weight
    return (weight - rate * update, new_moment, new_second)


def square_sum(values):
    return jnp.sum(values * values)


def gathered_total(flat_value, axis_names):
    columns = -(-flat_value.size // 1024) * 128
    block = jnp.pad(flat_value, (0, 8 * columns - flat_value.size)).reshape(8, columns)
    blocks = lax.all_gather(block, axis_names, axis=0, tiled=True)
    return jnp.sum(blocks.reshape(-1, 8, columns), axis=0).reshape(-1)


def exchange_total(part, bits, half_width):
    total = part
    for bit in bits:
        pairs = [(index, index ^ bit) for index in range(lax.axis_size("tensor"))]
        if half_width:
            rounded = lax.reduce_precision(total, 8, 7)
            other = lax.ppermute(rounded.astype(jnp.bfloat16), "tensor", pairs)
            total = rounded.astype(jnp.float32) + other.astype(jnp.float32)
        else:
            total = total + lax.ppermute(total, "tensor", pairs)
    return total


def tensor_total(partial_value, half_width=True):
    tensor_count = lax.axis_size("tensor")
    if tensor_count & (tensor_count - 1):
        return lax.psum(partial_value, "tensor")
    bits = [1 << place for place in range(tensor_count.bit_length() - 1)]
    if not half_width:
        return exchange_total(partial_value, bits, False)
    middle_row = partial_value.shape[0] // 2
    return jnp.concatenate(
        [
            exchange_total(partial_value[:middle_row], bits, True),
            exchange_total(partial_value[middle_row:], bits[::-1], True),
        ],
        axis=0,
    )


def body(
    inputs,
    cotangent,
    norm_gains,
    mix_weight,
    gate_weight,
    conv_weight,
    a_log,
    dt_bias,
    out_gain,
    out_weight,
    upgate_weight,
    down_weight,
    moment_norm_gains,
    moment_mix_weight,
    moment_gate_weight,
    moment_conv_weight,
    moment_a_log,
    moment_dt_bias,
    moment_out_gain,
    moment_out_weight,
    moment_upgate_weight,
    moment_down_weight,
    second_norm_gains,
    second_mix_weight,
    second_gate_weight,
    second_conv_weight,
    second_a_log,
    second_dt_bias,
    second_out_gain,
    second_out_weight,
    second_upgate_weight,
    second_down_weight,
):
    owned_rows = mix_weight.shape[0]
    head_count = mix_weight.shape[1]
    hidden_count = upgate_weight.shape[2]
    mix_columns = mix_weight.size // owned_rows
    gate_columns = gate_weight.size // owned_rows
    joint_shard = jnp.concatenate(
        [
            mix_weight.astype(jnp.bfloat16).reshape(owned_rows, -1),
            gate_weight.astype(jnp.bfloat16).reshape(owned_rows, -1),
            jnp.zeros((owned_rows, 128 - gate_columns), jnp.bfloat16),
        ],
        axis=1,
    )
    joint_full = lax.all_gather(joint_shard, "dp", axis=0, tiled=True)
    out_full = lax.all_gather(out_weight.astype(jnp.bfloat16), "dp", axis=2, tiled=True)
    upgate_full = lax.all_gather(
        upgate_weight.astype(jnp.bfloat16), "dp", axis=0, tiled=True
    )
    down_full = lax.all_gather(down_weight.astype(jnp.bfloat16), "dp", axis=1, tiled=True)
    row_count, model_width = inputs.shape
    seq_count = row_count // LEN
    normed_one = norm_apply(inputs, norm_gains[0]).astype(jnp.bfloat16)
    joint_in = jnp.dot(normed_one, joint_full, preferred_element_type=jnp.float32)
    mixed_in = jnp.swapaxes(
        joint_in[:, :mix_columns].reshape(seq_count, LEN, head_count, -1), 1, 2
    )
    gate_in = jnp.moveaxis(
        joint_in[:, mix_columns : mix_columns + gate_columns].reshape(
            seq_count, LEN, 2, head_count
        ),
        1,
        3,
    )
    core_out, core_back = jax.vjp(
        mixer_core, mixed_in, gate_in, conv_weight, a_log, dt_bias, out_gain
    )
    core_half = (
        jnp.swapaxes(core_out.astype(jnp.bfloat16), 1, 2).reshape(row_count, -1)
    )
    flat_out = out_full.reshape(-1, model_width)
    middle_part = jnp.dot(core_half, flat_out, preferred_element_type=jnp.float32)
    middle = inputs + tensor_total(middle_part)
    normed_rows = norm_apply(middle, norm_gains[1]).astype(jnp.bfloat16)
    flat_upgate = upgate_full.reshape(model_width, -1)
    paired = jnp.dot(normed_rows, flat_upgate, preferred_element_type=jnp.float32).reshape(
        row_count, 2, hidden_count
    )
    hidden_act, swiglu_back = jax.vjp(swiglu, paired)
    hidden_half = hidden_act.astype(jnp.bfloat16)
    cot_half = cotangent.astype(jnp.bfloat16)
    grad_hidden = jnp.dot(cot_half, down_full.T, preferred_element_type=jnp.float32)
    grad_paired = swiglu_back(grad_hidden)[0].reshape(row_count, -1).astype(jnp.bfloat16)
    grad_normed_two = tensor_total(
        jnp.dot(grad_paired, flat_upgate.T, preferred_element_type=jnp.float32)
    )
    output_part = jnp.dot(hidden_half, down_full, preferred_element_type=jnp.float32)
    grad_down = jnp.dot(
        hidden_half.T, cot_half, preferred_element_type=jnp.float32
    ).astype(jnp.bfloat16)
    grad_upgate = (
        jnp.dot(normed_rows.T, grad_paired, preferred_element_type=jnp.float32)
        .astype(jnp.bfloat16)
        .reshape(upgate_full.shape)
    )
    grad_normed_two, output_part = lax.optimization_barrier((grad_normed_two, output_part))
    shard_upgate = lax.psum_scatter(grad_upgate, "dp", scatter_dimension=0, tiled=True)
    shard_down = lax.psum_scatter(grad_down, "dp", scatter_dimension=1, tiled=True)
    output_total = tensor_total(output_part)
    norm_two_back = jax.vjp(norm_apply, middle, norm_gains[1])[1]
    grad_from_second, grad_gain_two = norm_two_back(grad_normed_two)
    grad_middle = cotangent + grad_from_second
    middle_rows = grad_middle.astype(jnp.bfloat16)
    grad_out = jnp.dot(core_half.T, middle_rows, preferred_element_type=jnp.float32).reshape(
        out_full.shape
    )
    shard_out = lax.psum_scatter(
        grad_out.astype(jnp.bfloat16), "dp", scatter_dimension=2, tiled=True
    )
    grad_core = jnp.swapaxes(
        jnp.dot(middle_rows, flat_out.T, preferred_element_type=jnp.float32).reshape(
            seq_count, LEN, head_count, -1
        ),
        1,
        2,
    )
    grad_mixed, grad_gate_in, grad_conv, grad_a_log_part, grad_dt_part, grad_gain_part = core_back(
        grad_core
    )
    joint_grad_half = jnp.concatenate(
        [
            jnp.swapaxes(grad_mixed.astype(jnp.bfloat16), 1, 2).reshape(row_count, -1),
            jnp.moveaxis(grad_gate_in.astype(jnp.bfloat16), 3, 1).reshape(row_count, -1),
            jnp.zeros((row_count, 128 - gate_columns), jnp.bfloat16),
        ],
        axis=1,
    )
    partial_first = jnp.dot(
        joint_grad_half, joint_full.T, preferred_element_type=jnp.float32
    )
    output_rows = middle + output_total
    shard_upgate, shard_down, shard_out = (
        shard_upgate.astype(jnp.float32),
        shard_down.astype(jnp.float32),
        shard_out.astype(jnp.float32),
    )
    grad_normed_one = tensor_total(partial_first)
    grad_joint = jnp.dot(normed_one.T, joint_grad_half, preferred_element_type=jnp.float32)
    shard_joint = lax.psum_scatter(
        grad_joint.astype(jnp.bfloat16), "dp", scatter_dimension=0, tiled=True
    ).astype(jnp.float32)
    shard_mix = shard_joint[:, :mix_columns].reshape(mix_weight.shape)
    shard_gate = shard_joint[:, mix_columns : mix_columns + gate_columns].reshape(
        gate_weight.shape
    )
    norm_one_back = jax.vjp(norm_apply, inputs, norm_gains[0])[1]
    grad_from_first, grad_gain_one = norm_one_back(grad_normed_one)
    grad_input_rows = grad_middle + grad_from_first
    dp_count = lax.axis_size("dp")
    tensor_count = lax.axis_size("tensor")
    early = jnp.concatenate(
        [
            grad_conv.reshape(-1),
            grad_gain_two.reshape(-1),
            grad_a_log_part.reshape(-1),
            grad_dt_part.reshape(-1),
        ]
    )
    early = gathered_total(early, "dp")
    cut = [grad_conv.size, model_width, a_log.size, dt_bias.size]
    grad_conv_weight = early[: cut[0]].reshape(conv_weight.shape)
    grad_gain_two = early[cut[0] : cut[0] + cut[1]]
    grad_a_log = early[cut[0] + cut[1] : cut[0] + cut[1] + cut[2]]
    grad_dt_bias = early[cut[0] + cut[1] + cut[2] : sum(cut)]
    local_squares = jnp.stack(
        [
            square_sum(shard_mix),
            square_sum(shard_gate),
            square_sum(shard_out),
            square_sum(shard_upgate),
            square_sum(shard_down),
            square_sum(grad_conv_weight) / dp_count,
            square_sum(grad_a_log) / dp_count,
            square_sum(grad_dt_bias) / dp_count,
        ]
    )
    late = jnp.concatenate([grad_gain_one / tensor_count, grad_gain_part, local_squares])
    late = gathered_total(tensor_total(late, False), "dp")
    grad_norm_gains = jnp.stack([late[:model_width], grad_gain_two])
    grad_out_gain = late[model_width : model_width + out_gain.size]
    total_squares = late[model_width + out_gain.size : model_width + out_gain.size + 8]
    spread = dp_count * tensor_count
    new_norm_gains, new_moment_norm_gains, new_second_norm_gains = adamw_update(
        norm_gains,
        grad_norm_gains,
        moment_norm_gains,
        second_norm_gains,
        RATE_VECTOR,
        square_sum(grad_norm_gains),
        grad_norm_gains.size,
    )
    new_mix_weight, new_moment_mix_weight, new_second_mix_weight = adamw_update(
        mix_weight,
        shard_mix,
        moment_mix_weight,
        second_mix_weight,
        RATE_MATRIX,
        total_squares[0],
        shard_mix.size * spread,
    )
    new_gate_weight, new_moment_gate_weight, new_second_gate_weight = adamw_update(
        gate_weight,
        shard_gate,
        moment_gate_weight,
        second_gate_weight,
        RATE_MATRIX,
        total_squares[1],
        shard_gate.size * spread,
    )
    new_conv_weight, new_moment_conv_weight, new_second_conv_weight = adamw_update(
        conv_weight,
        grad_conv_weight,
        moment_conv_weight,
        second_conv_weight,
        RATE_VECTOR,
        total_squares[5],
        grad_conv_weight.size * tensor_count,
    )
    new_a_log, new_moment_a_log, new_second_a_log = adamw_update(
        a_log,
        grad_a_log,
        moment_a_log,
        second_a_log,
        RATE_VECTOR,
        total_squares[6],
        grad_a_log.size * tensor_count,
    )
    new_dt_bias, new_moment_dt_bias, new_second_dt_bias = adamw_update(
        dt_bias,
        grad_dt_bias,
        moment_dt_bias,
        second_dt_bias,
        RATE_VECTOR,
        total_squares[7],
        grad_dt_bias.size * tensor_count,
    )
    new_out_gain, new_moment_out_gain, new_second_out_gain = adamw_update(
        out_gain,
        grad_out_gain,
        moment_out_gain,
        second_out_gain,
        RATE_VECTOR,
        square_sum(grad_out_gain),
        grad_out_gain.size,
    )
    new_out_weight, new_moment_out_weight, new_second_out_weight = adamw_update(
        out_weight,
        shard_out,
        moment_out_weight,
        second_out_weight,
        RATE_MATRIX,
        total_squares[2],
        shard_out.size * spread,
    )
    new_upgate_weight, new_moment_upgate_weight, new_second_upgate_weight = adamw_update(
        upgate_weight,
        shard_upgate,
        moment_upgate_weight,
        second_upgate_weight,
        RATE_MATRIX,
        total_squares[3],
        shard_upgate.size * spread,
    )
    new_down_weight, new_moment_down_weight, new_second_down_weight = adamw_update(
        down_weight,
        shard_down,
        moment_down_weight,
        second_down_weight,
        RATE_MATRIX,
        total_squares[4],
        shard_down.size * spread,
    )
    return (
        output_rows,
        grad_input_rows,
        grad_norm_gains,
        shard_mix,
        shard_gate,
        grad_conv_weight,
        grad_a_log,
        grad_dt_bias,
        grad_out_gain,
        shard_out,
        shard_upgate,
        shard_down,
        new_norm_gains,
        new_mix_weight,
        new_gate_weight,
        new_conv_weight,
        new_a_log,
        new_dt_bias,
        new_out_gain,
        new_out_weight,
        new_upgate_weight,
        new_down_weight,
        new_moment_norm_gains,
        new_moment_mix_weight,
        new_moment_gate_weight,
        new_moment_conv_weight,
        new_moment_a_log,
        new_moment_dt_bias,
        new_moment_out_gain,
        new_moment_out_weight,
        new_moment_upgate_weight,
        new_moment_down_weight,
        new_second_norm_gains,
        new_second_mix_weight,
        new_second_gate_weight,
        new_second_conv_weight,
        new_second_a_log,
        new_second_dt_bias,
        new_second_out_gain,
        new_second_out_weight,
        new_second_upgate_weight,
        new_second_down_weight,
    )


def solution(mesh):
    placed = (
        P("dp", None),
        P("dp", None),
        P(),
        P("dp", "tensor", None),
        P("dp", None, "tensor"),
        P(None, "tensor", None),
        P("tensor"),
        P("tensor"),
        P(),
        P("tensor", None, "dp"),
        P("dp", None, "tensor"),
        P("tensor", "dp"),
        P(),
        P("dp", "tensor", None),
        P("dp", None, "tensor"),
        P(None, "tensor", None),
        P("tensor"),
        P("tensor"),
        P(),
        P("tensor", None, "dp"),
        P("dp", None, "tensor"),
        P("tensor", "dp"),
        P(),
        P("dp", "tensor", None),
        P("dp", None, "tensor"),
        P(None, "tensor", None),
        P("tensor"),
        P("tensor"),
        P(),
        P("tensor", None, "dp"),
        P("dp", None, "tensor"),
        P("tensor", "dp"),
    )
    return jax.shard_map(
        body,
        mesh=mesh,
        in_specs=placed,
        out_specs=(
            P("dp", None),
            P("dp", None),
            P(),
            P("dp", "tensor", None),
            P("dp", None, "tensor"),
            P(None, "tensor", None),
            P("tensor"),
            P("tensor"),
            P(),
            P("tensor", None, "dp"),
            P("dp", None, "tensor"),
            P("tensor", "dp"),
            P(),
            P("dp", "tensor", None),
            P("dp", None, "tensor"),
            P(None, "tensor", None),
            P("tensor"),
            P("tensor"),
            P(),
            P("tensor", None, "dp"),
            P("dp", None, "tensor"),
            P("tensor", "dp"),
            P(),
            P("dp", "tensor", None),
            P("dp", None, "tensor"),
            P(None, "tensor", None),
            P("tensor"),
            P("tensor"),
            P(),
            P("tensor", None, "dp"),
            P("dp", None, "tensor"),
            P("tensor", "dp"),
            P(),
            P("dp", "tensor", None),
            P("dp", None, "tensor"),
            P(None, "tensor", None),
            P("tensor"),
            P("tensor"),
            P(),
            P("tensor", None, "dp"),
            P("dp", None, "tensor"),
            P("tensor", "dp"),
        ),
        check_vma=False,
    )
```
